32 devices in a mesh: ens: 2 (over y), lon: 4 (over z), lat: 4 (over x, core).
Axes of the slice: x: 2, y: 2, z: 4, core: 2. Of those that a mesh axis runs over, the one named last changes fastest.
Arguments:
- tracers: float32 [8, 16, 2048], P('ens', 'lat', 'lon'), parts along dimension 0, may hold values from -6 to 6
- forcing: float32 [8, 16, 2048], P('ens', 'lat', 'lon'), parts along dimension 0, may hold values from -4 to 4
- diffusivity: float32 [16, 2048], P('lat', 'lon'), may hold values from 0.02 to 0.2
- ocean_mask: int32 [16, 2048], P('lat', 'lon'), may hold values 0 or 1
- weight_in: bfloat16 [32, 4, 3, 3], replicated, may hold values from -1 to 1
- weight_mid: bfloat16 [32, 32, 3, 3], replicated, may hold values from -0.375 to 0.375
- weight_out: bfloat16 [4, 32, 3, 3], replicated, may hold values from -0.375 to 0.375
- sensitivity: float32 [8, 16, 2048], P('ens', 'lat', 'lon'), parts along dimension 0, may hold values from -6 to 6
Outputs:
- final_tracers: float32 [8, 16, 2048], P('ens', 'lat', 'lon'), parts along dimension 0
- gradient_in: float32 [64, 4, 3, 3], P('ens'), parts along dimension 0
- gradient_mid: float32 [64, 32, 3, 3], P('ens'), parts along dimension 0
- gradient_out: float32 [8, 32, 3, 3], P('ens'), parts along dimension 0
The draws below stay inside these ranges and needn't reach their ends.
There are 2 independent parts, one for each index of `ens`. The reference program is written for one: setup_inputs(seed, part) draws one part's arguments, and reference() takes and returns one part's arrays. A program takes and returns all parts, laid end to end along the dimension named above; an argument that names none is the same for every part. Nothing has to cross between parts.
All inputs are finite; a program needn't handle non-finite values. No bound on the sum of `ocean_mask` on one device may be relied on, other than what follows from the above.
Results may differ from the reference program's by a relative error of at most 0.0065.
Values may be sent and summed in bfloat16 or wider, within the bound.
A program may use at most 64 MiB of HBM per device.

```python
import math
import jax
import jax.numpy as jnp
from jax import lax

C = 4
HID = 32
NX = 2048
NY = 16


def touch_ends(entries, key, least, top_value):
    place = [jax.random.randint(jax.random.fold_in(key, axis), (), 0, length) for axis, length in enumerate(entries.shape)]
    widest = entries.shape.index(max(entries.shape))
    next_to = place[:widest] + [(place[widest] + 1) % entries.shape[widest]] + place[widest + 1:]
    return entries.at[tuple(place)].set(least).at[tuple(next_to)].set(top_value)


def shard_levels(key, dims, cuts, least, top_value):
    loudness, own = 1.0, jax.random.fold_in(key, 6)
    for dim, blocks in cuts:
        steps = jnp.exp(jax.random.uniform(jax.random.fold_in(own, dim), (blocks,), jnp.float32, least / len(cuts), top_value / len(cuts)))
        loudness = loudness * jnp.repeat(steps, dims[dim] // blocks).reshape([-1 if axis == dim else 1 for axis in range(len(dims))])
    return loudness


def normal_values(key, shape, deviation, reach, cuts=(), held_as=jnp.bfloat16):
    array = jax.random.normal(key, shape, jnp.float32) * deviation
    if len(cuts) > 0:
        array = shard_levels(key, shape, cuts, -0.22, 0.18) * array
    return jnp.clip(array, min=-reach, max=reach).astype(held_as)


def setup_inputs(seed: int = 0, part: int = 0) -> dict:
    arg_keys = jax.random.split(jax.random.key(seed), 9)
    part_splits = jax.random.split(jax.random.fold_in(arg_keys[8], part), 9)
    return {
        "tracers": normal_values(part_splits[0], (C, NY, NX), 1.0, 6.0, ((1, 4), (2, 4)), jnp.float32),
        "forcing": normal_values(part_splits[1], (C, NY, NX), 0.5, 4.0, ((1, 4), (2, 4)), jnp.float32),
        "diffusivity": jnp.clip(jnp.exp(math.log(0.2) - 2.3025851 * jax.random.uniform(arg_keys[2], (NY, NX), jnp.float32) ** shard_levels(arg_keys[2], (NY, NX), ((0, 4), (1, 4)), -0.2, 0.2)), 0.02, 0.2),
        "ocean_mask": touch_ends((jax.random.randint(arg_keys[3], (NY, NX), 0, 10) < 7).astype(jnp.int32), jax.random.fold_in(arg_keys[3], 1), 0, 1),
        "weight_in": normal_values(arg_keys[4], (HID, C, 3, 3), (9 * C) ** -0.5, 1.0),
        "weight_mid": normal_values(arg_keys[5], (HID, HID, 3, 3), (9 * HID) ** -0.5, 0.375),
        "weight_out": normal_values(arg_keys[6], (C, HID, 3, 3), (9 * HID) ** -0.5, 0.375),
        "sensitivity": normal_values(part_splits[7], (C, NY, NX), 1.0, 6.0, ((1, 4), (2, 4)), jnp.float32),
    }


CLOSURE_GAIN = 0.5

def pad_field(field, rim_width):
    wrapped = jnp.pad(field, ((0, 0), (0, 0), (rim_width, rim_width)), mode='wrap')
    return jnp.pad(wrapped, ((0, 0), (rim_width, rim_width), (0, 0)))

def conv_valid(padded, weight):
    height = padded.shape[1] - 2
    breadth = padded.shape[2] - 2
    weight_f = weight.astype(jnp.float32)
    result = None
    for row_off in range(3):
        for col_off in range(3):
            window = padded[:, row_off:row_off + height, col_off:col_off + breadth].astype(jnp.float32)
            product = lax.dot_general(weight_f[:, :, row_off, col_off], window, (((1,), (0,)), ((), ())), precision=lax.Precision.HIGHEST)
            result = product if result is None else result + product
    return result

def flipped(weight):
    return jnp.flip(weight, (2, 3)).transpose(1, 0, 2, 3)

def slope(hidden):
    return 1.0 - jnp.square(hidden.astype(jnp.float32))

def kernel_grad(padded, cotangent):
    height = cotangent.shape[1]
    breadth = cotangent.shape[2]
    cot_f = cotangent.astype(jnp.float32)
    pieces = []
    for row_off in range(3):
        for col_off in range(3):
            window = padded[:, row_off:row_off + height, col_off:col_off + breadth].astype(jnp.float32)
            pieces.append(lax.dot_general(cot_f, window, (((1, 2), (1, 2)), ((), ())), precision=lax.Precision.HIGHEST))
    stacked = jnp.stack(pieces, 0)
    return stacked.reshape(3, 3, stacked.shape[1], stacked.shape[2]).transpose(2, 3, 0, 1)

def laplace(padded):
    return padded[:, 2:, 1:-1] + padded[:, :-2, 1:-1] + padded[:, 1:-1, 2:] + padded[:, 1:-1, :-2] - 4.0 * padded[:, 1:-1, 1:-1]

def reference(tracers, forcing, diffusivity, ocean_mask, weight_in, weight_mid, weight_out, sensitivity):
    sea_cells = ocean_mask.astype(jnp.float32)[None]
    kappa_cells = diffusivity[None]
    state_now = tracers
    saved = []
    for step in range(2):
        state_pad = pad_field(state_now, 1)
        source_pad = state_pad.astype(jnp.bfloat16)
        hidden_one = jnp.tanh(conv_valid(source_pad, weight_in)).astype(jnp.bfloat16)
        first_pad = pad_field(hidden_one, 1)
        hidden_two = jnp.tanh(conv_valid(first_pad, weight_mid)).astype(jnp.bfloat16)
        second_pad = pad_field(hidden_two, 1)
        closure = conv_valid(second_pad, weight_out)
        state_now = sea_cells * (state_now + kappa_cells * laplace(state_pad) + CLOSURE_GAIN * closure + forcing)
        saved.append((source_pad, first_pad, second_pad))
    adjoint = sensitivity
    grad_one = None
    for step in (1, 0):
        source_pad, first_pad, second_pad = saved[step]
        masked_cot = sea_cells * adjoint
        closure_cot = (CLOSURE_GAIN * masked_cot).astype(jnp.bfloat16)
        second_core = second_pad[:, 1:-1, 1:-1]
        first_core = first_pad[:, 1:-1, 1:-1]
        lower_two = (conv_valid(pad_field(closure_cot, 1), flipped(weight_out)) * slope(second_core)).astype(jnp.bfloat16)
        lower_one = (conv_valid(pad_field(lower_two, 1), flipped(weight_mid)) * slope(first_core)).astype(jnp.bfloat16)
        part_three = kernel_grad(second_pad, closure_cot)
        part_two = kernel_grad(first_pad, lower_two)
        part_one = kernel_grad(source_pad, lower_one)
        if grad_one is None:
            grad_one, grad_two, grad_three = (part_one, part_two, part_three)
        else:
            grad_one = grad_one + part_one
            grad_two = grad_two + part_two
            grad_three = grad_three + part_three
        if step == 1:
            adjoint = masked_cot + laplace(pad_field(kappa_cells * masked_cot, 1)) + conv_valid(pad_field(lower_one, 1), flipped(weight_in))
    norm_scale = 1.0 / math.sqrt(NX * NY)
    return (state_now, grad_one * norm_scale, grad_two * norm_scale, grad_three * norm_scale)
```

```python
import functools
import math

import jax
import jax.numpy as jnp
import numpy as np
from jax import lax
from jax.experimental import pallas as pl
from jax.experimental.pallas import tpu as pltpu
from jax.sharding import PartitionSpec as P

GAIN = 0.5
MESH = pl.DeviceIdType.MESH
F32 = jnp.float32
BF16 = jnp.bfloat16
TILE = 128
WIDE = 256
HID = 32
DEEP = 3 * HID
GROUP = 4
OWN_ROWS = 16


def dot(a, b):
    return jnp.dot(a, b, preferred_element_type=F32)


def dot_nt(a, b):
    return lax.dot_general(a, b, (((1,), (1,)), ((), ())), preferred_element_type=F32)


def left_of(v):
    return pltpu.roll(v, 1, 1)


def right_of(v):
    return pltpu.roll(v, WIDE - 1, 1)


def spread_matrix():
    m = np.zeros((80, 64), np.float32)
    for r in range(4):
        for c in range(4):
            for k in range(3):
                m[k * 16 + r * 4 + c, k * 16 + c * 4 + r] = 1
            m[48 + r * 4 + c, 48 + r] = 1
            m[64 + r * 4 + c, 52 + r] = 1
    return m


def kernel(
    n_lat, n_lon, halo, scale,
    tr_ref, fo_ref, ka_ref, ma_ref, wi_ref, wm_ref, wo_ref, se_ref, sp_ref,
    final_ref, gin_ref, gmid_ref, gout_ref,
    pk, rbuf, st, fo, se, ka, ma, lap, sixteen,
    t_if, t_ib, t_mf, t_mb, t_of, t_ob, t_tmp, t_wide,
    src, cc, h1, h2, l2, l1, acc, chunk, rs, total, fsrc, fdst,
    x_send, x_recv, f_send, f_recv, rs_send, rs_recv, ag_send, ag_recv,
):
    lat = lax.axis_index("lat")
    lon = lax.axis_index("lon")
    group = lat // GROUP
    j = lat % GROUP
    n_groups = n_lat // GROUP
    blocks = GROUP + 2 * halo
    rows = 4 * blocks
    reduce_here = n_lat * n_lon == 16

    barrier = pltpu.get_barrier_semaphore()
    if reduce_here:
        peers = [(dl, dz) for dz in range(n_lon) for dl in range(n_lat) if (dl, dz) != (0, 0)]
        peer_ids = [((lat + dl) % n_lat, (lon + dz) % n_lon) for dl, dz in peers]
    else:
        peer_ids = []
        for dg in (-1, 0, 1):
            for dj in range(GROUP):
                for dz in (-1, 0, 1):
                    if (dg, dj, dz) != (0, 0, 0):
                        other = (group + dg + n_groups) % n_groups
                        peer_ids.append((other * GROUP + (j + dj) % GROUP, (lon + dz + n_lon) % n_lon))
    for pl_lat, pl_lon in peer_ids:
        pl.semaphore_signal(
            barrier, inc=1, device_id={"lat": pl_lat, "lon": pl_lon}, device_id_type=MESH
        )

    pieces = [tr_ref[c] for c in range(4)] + [fo_ref[c] for c in range(4)] + [se_ref[c] for c in range(4)]
    pieces += [ka_ref[...], ma_ref[...].astype(F32)]
    for i, piece in enumerate(pieces):
        t_wide[i * 4 : i * 4 + 4, :] = piece
    t_wide[56:64, :] = jnp.zeros((8, 512), F32)
    packed = t_wide[...].astype(BF16)
    for t in range(GROUP):
        pk[t] = packed[:, t * TILE : (t + 1) * TILE]

    pl.semaphore_wait(barrier, len(peer_ids))

    waits = []

    def send(tile, slot, which, sem, to_lat, to_lon, when):
        copy = pltpu.make_async_remote_copy(
            src_ref=pk.at[tile],
            dst_ref=rbuf.at[slot, which],
            send_sem=x_send.at[sem],
            recv_sem=x_recv.at[slot, which],
            device_id={"lat": to_lat, "lon": to_lon},
            device_id_type=MESH,
        )
        if when is None:
            copy.start()
        else:
            pl.when(when)(copy.start)
        waits.append((copy, when))

    def keep(tile, slot, which, when):
        copy = pltpu.make_async_copy(pk.at[tile], rbuf.at[slot, which], x_recv.at[slot, which])
        if when is None:
            copy.start()
        else:
            pl.when(when)(copy.start)

    number = 0
    for dg in (0,) if halo == 0 else (-1, 0, 1):
        gate = None if dg == 0 else (j >= 1 if dg == 1 else j <= 2)
        to_group = ((group + dg + n_groups) % n_groups) * GROUP
        slot = j - 4 * dg + halo
        for s in (1, 2, 3, 0):
            t = (j + s) % GROUP
            own = dg == 0
            if own and s == 0:
                keep(t, slot, 1, None)
            else:
                send(t, slot, 1, number, to_group + t, lon, gate)
            number += 1
            if own and s == 3:
                keep(t, slot, 0, t != 3)
                when = t == 3
            else:
                when = gate
            send(
                t, slot, 0, number, to_group + (t + 1) % GROUP,
                (lon + (t == 3).astype(jnp.int32)) % n_lon, when,
            )
            number += 1
            if own and s == 1:
                keep(t, slot, 2, t != 0)
                when = t == 0
            else:
                when = gate
            send(
                t, slot, 2, number, to_group + (t + 3) % GROUP,
                (lon + n_lon - (t == 0).astype(jnp.int32)) % n_lon, when,
            )
            number += 1

    def banded_wide(parts, out_rows, target):
        t_tmp[...] = jnp.zeros_like(t_tmp)
        strip = jnp.concatenate(parts, axis=1)
        for r in range(4):
            t_tmp[r * out_rows : (r + 1) * out_rows, r * DEEP : r * DEEP + 3 * DEEP] = strip
        target[...] = t_tmp[0 : 4 * out_rows, 0 : 6 * DEEP].astype(BF16)

    def banded_narrow(parts, target):
        t_tmp[0:128, 0:128] = jnp.zeros((128, 128), F32)
        for r in range(4):
            for a in range(3):
                for b in range(3):
                    top = (r + a) * 16 + b * 4
                    t_tmp[top : top + 4, r * HID : (r + 1) * HID] = parts[a * 3 + b]
        target[...] = jnp.transpose(t_tmp[0:128, 0:128])[:, 0:96].astype(BF16)

    wi = [wi_ref[k].astype(F32) for k in range(9)]
    wm = [wm_ref[k].astype(F32) for k in range(9)]
    wo = [wo_ref[k].astype(F32) for k in range(9)]
    banded_narrow(wi, t_if)
    banded_wide(wm, HID, t_mf)
    banded_wide(wo, 4, t_of)
    banded_narrow(wo[::-1], t_ob)
    banded_wide([jnp.transpose(w) for w in wm[::-1]], HID, t_mb)
    banded_wide(wi[::-1], 4, t_ib)

    for buf in (h1, h2, l2, l1):
        for n in range(2):
            buf[n, 0:DEEP, :] = jnp.zeros((DEEP, WIDE), BF16)
            buf[n, (rows + 1) * DEEP : (rows + 2) * DEEP, :] = jnp.zeros((DEEP, WIDE), BF16)
    for buf in (src, cc):
        for n in range(2):
            buf[n, 0:16, :] = jnp.zeros((16, WIDE), BF16)
            buf[n, (rows + 1) * 16 : (rows + 2) * 16, :] = jnp.zeros((16, WIDE), BF16)
    sixteen[...] = jnp.zeros_like(sixteen)
    lap[...] = jnp.zeros_like(lap)

    def inside(per_row, count, first):
        if halo == 0:
            return None
        at = lax.broadcasted_iota(jnp.int32, (count, WIDE), 0) // per_row + first
        at = at + (group * GROUP - halo) * 4
        return ((at >= 0) & (at < n_lat * 4)).astype(F32)

    def clear(v, per_row, first):
        if halo == 0:
            return v
        return v * inside(per_row, v.shape[0], first)

    lane = lax.broadcasted_iota(jnp.int32, (80, TILE), 1)
    for w in range(blocks):
        for which in range(3):
            pltpu.make_async_copy(pk.at[0], rbuf.at[w, which], x_recv.at[w, which]).wait()
    for w in range(blocks):
        three = jnp.concatenate([rbuf[w, 1], rbuf[w, 0], rbuf[w, 2]], axis=1)
        got = dot(sp_ref[...], three)
        side = jnp.where(lane < TILE // 2, got[:, 2 * TILE :], got[:, TILE : 2 * TILE])
        both = jnp.concatenate([got[:, 0:TILE], side], axis=1)
        here = slice(w * 16, (w + 1) * 16)
        st[here, :] = clear(both[0:16], 4, 4 * w)
        fo[here, :] = both[16:32]
        se[here, :] = both[32:48]
        ka[here, :] = both[48:64]
        ma[here, :] = clear(both[64:80], 4, 4 * w)

    def put_narrow(target, n, v):
        for b, moved in enumerate((left_of(v), v, right_of(v))):
            for r in range(rows):
                sixteen[r * 16 + b * 4 : r * 16 + b * 4 + 4, :] = moved[r * 4 : r * 4 + 4]
        target[n, 16 : 16 + rows * 16, :] = sixteen[...].astype(BF16)

    def put_wide(target, n, w, v):
        v = clear(v, HID, 4 * w)
        for b, moved in enumerate((left_of(v), v, right_of(v))):
            moved = moved.astype(BF16)
            for r in range(4):
                top = (4 * w + r + 1) * DEEP + b * HID
                target[n, top : top + HID, :] = moved[r * HID : (r + 1) * HID]

    def centre(target, n, w):
        parts = []
        for r in range(4):
            top = (4 * w + r + 1) * DEEP + HID
            parts.append(target[n, top : top + HID, :])
        return jnp.concatenate(parts, axis=0).astype(F32)

    def narrow_window(target, n, w):
        return target[n, w * 64 : w * 64 + 96, :]

    def wide_window(target, n, w):
        return target[n, 4 * w * DEEP : 4 * w * DEEP + 6 * DEEP, :]

    def laplace(v):
        lap[8 : 8 + rows * 4, :] = v
        up = lap[4 : 4 + rows * 4, :]
        down = lap[12 : 12 + rows * 4, :]
        return up + down + left_of(v) + right_of(v) - 4.0 * v

    def forward(n, state):
        put_narrow(src, n, state)
        for w in range(blocks):
            put_wide(h1, n, w, jnp.tanh(dot(t_if[...], narrow_window(src, n, w))))
        for w in range(blocks):
            put_wide(h2, n, w, jnp.tanh(dot(t_mf[...], wide_window(h1, n, w))))
        closure = jnp.concatenate(
            [dot(t_of[...], wide_window(h2, n, w)) for w in range(blocks)], axis=0
        )
        return ma[...] * (state + ka[...] * laplace(state) + GAIN * closure + fo[...])

    def strip_wide(target, n):
        parts = []
        for s in range(OWN_ROWS + 2):
            top = (4 * halo + s) * DEEP
            parts.append(target[n, top : top + DEEP, 0:TILE])
        return jnp.concatenate(parts, axis=1)

    def strip_narrow(target, n):
        parts = []
        for s in range(OWN_ROWS + 2):
            top = (4 * halo + s) * 16
            parts.append(target[n, top : top + 16, 0:TILE])
        return jnp.concatenate(parts, axis=1)

    def strip_shifted(read, height):
        zero = jnp.zeros((height, TILE), BF16)
        cells = [read(r) for r in range(OWN_ROWS)]
        return jnp.concatenate(
            [jnp.concatenate([zero] * a + cells + [zero] * (2 - a), axis=1) for a in range(3)],
            axis=0,
        )

    def read_wide(target, n):
        def read(r):
            top = (4 * halo + r + 1) * DEEP + HID
            return target[n, top : top + HID, 0:TILE]

        return read

    def read_narrow(target, n):
        def read(r):
            top = (4 * halo + r + 1) * 16
            return target[n, top : top + 16, 0:TILE]

        return read

    def backward(n, masked, need_state):
        put_narrow(cc, n, GAIN * masked)
        grad_out = dot_nt(strip_shifted(read_narrow(cc, n), 16), strip_wide(h2, n))
        for w in range(blocks):
            slope = 1.0 - jnp.square(centre(h2, n, w))
            put_wide(l2, n, w, dot(t_ob[...], narrow_window(cc, n, w)) * slope)
        grad_mid = dot_nt(strip_shifted(read_wide(l2, n), HID), strip_wide(h1, n))
        for w in range(blocks):
            slope = 1.0 - jnp.square(centre(h1, n, w))
            put_wide(l1, n, w, dot(t_mb[...], wide_window(l2, n, w)) * slope)
        grad_in = dot_nt(strip_narrow(src, n), strip_shifted(read_wide(l1, n), HID))
        earlier = None
        if need_state:
            through = jnp.concatenate(
                [dot(t_ib[...], wide_window(l1, n, w)) for w in range(blocks)], axis=0
            )
            earlier = masked + laplace(ka[...] * masked) + through
        return earlier, (grad_in, grad_mid, grad_out)

    state = forward(0, st[...])
    final = forward(1, state)
    for i in range(GROUP):
        top = (halo + i) * 16
        fsrc[i] = final[top : top + 16, 0:TILE]
    for s in (1, 2, 3):
        i = (j + s) % GROUP
        copy = pltpu.make_async_remote_copy(
            src_ref=fsrc.at[i],
            dst_ref=fdst.at[j],
            send_sem=f_send.at[s],
            recv_sem=f_recv.at[j],
            device_id={"lat": group * GROUP + i, "lon": lon},
            device_id_type=MESH,
        )
        copy.start()
        waits.append((copy, None))
    pltpu.make_async_copy(fsrc.at[j], fdst.at[j], f_recv.at[j]).start()

    adjoint, late = backward(1, ma[...] * se[...], True)
    _, early = backward(0, ma[...] * adjoint, False)

    g_in, g_mid, g_out = (a + b for a, b in zip(late, early))
    acc[...] = jnp.zeros_like(acc)
    acc[0:96, 0:96] = g_mid * scale
    for a in range(3):
        acc[96 + a * 4 : 100 + a * 4, 0:96] = g_out[a * 16 + 4 : a * 16 + 8] * scale
    acc[108:120, 0:96] = g_in[0:12] * scale

    if reduce_here:
        rank = lon * n_lat + lat
        sums = []
        for o, (to_lat, to_lon) in enumerate(peer_ids):
            other = to_lon * n_lat + to_lat
            copy = pltpu.make_async_remote_copy(
                src_ref=acc.at[pl.ds(pl.multiple_of(other * 8, 8), 8)],
                dst_ref=rs.at[o],
                send_sem=rs_send.at[o],
                recv_sem=rs_recv.at[o],
                device_id={"lat": to_lat, "lon": to_lon},
                device_id_type=MESH,
            )
            copy.start()
            waits.append((copy, None))
            sums.append(copy)
        mine = pl.ds(pl.multiple_of(rank * 8, 8), 8)
        whole = acc[mine, :]
        for o, copy in enumerate(sums):
            copy.wait_recv()
            whole = whole + rs[o]
        chunk[...] = whole
        total[mine, :] = whole
        gathered = []
        for o, (to_lat, to_lon) in enumerate(peer_ids):
            copy = pltpu.make_async_remote_copy(
                src_ref=chunk,
                dst_ref=total.at[mine],
                send_sem=ag_send.at[o],
                recv_sem=ag_recv.at[o],
                device_id={"lat": to_lat, "lon": to_lon},
                device_id_type=MESH,
            )
            copy.start()
            waits.append((copy, None))
            gathered.append(copy)

    for i in range(GROUP):
        pltpu.make_async_copy(fsrc.at[0], fdst.at[i], f_recv.at[i]).wait()
    for i in range(GROUP):
        for r in range(4):
            final_ref[r, :, i * TILE : (i + 1) * TILE] = fdst[i, r * 4 : r * 4 + 4, :]

    if reduce_here:
        for copy in gathered:
            copy.wait_recv()
        result = total[...]
    else:
        result = acc[...]
    for a in range(3):
        for b in range(3):
            k = a * 3 + b
            side = slice(b * HID, (b + 1) * HID)
            gmid_ref[k] = result[a * HID : (a + 1) * HID, side]
            gout_ref[k] = result[96 + a * 4 : 100 + a * 4, side]
            gin_ref[k] = result[108 + b * 4 : 112 + b * 4, a * HID : (a + 1) * HID]

    for copy, when in waits:
        if when is None:
            copy.wait_send()
        else:
            pl.when(when)(copy.wait_send)


def on_device(
    n_lat, n_lon,
    tracers, forcing, diffusivity, ocean_mask, weight_in, weight_mid, weight_out, sensitivity,
):
    halo = 0 if n_lat == GROUP else 3
    blocks = GROUP + 2 * halo
    rows = 4 * blocks
    scale = 1.0 / math.sqrt(tracers.shape[1] * n_lat * tracers.shape[2] * n_lon)
    vmem = pl.BlockSpec(memory_space=pltpu.VMEM)
    sends = 12 if halo == 0 else 36
    wi = weight_in.transpose(2, 3, 1, 0).reshape(9, 4, HID)
    wm = weight_mid.transpose(2, 3, 0, 1).reshape(9, HID, HID)
    wo = weight_out.transpose(2, 3, 0, 1).reshape(9, 4, HID)
    field = pltpu.VMEM((rows * 4, WIDE), F32)
    wide = pltpu.VMEM((2, (rows + 2) * DEEP, WIDE), BF16)
    narrow = pltpu.VMEM((2, (rows + 2) * 16, WIDE), BF16)
    final, g_in, g_mid, g_out = pl.pallas_call(
        functools.partial(kernel, n_lat, n_lon, halo, scale),
        out_shape=(
            jax.ShapeDtypeStruct((4, 4, 512), F32),
            jax.ShapeDtypeStruct((9, 4, HID), F32),
            jax.ShapeDtypeStruct((9, HID, HID), F32),
            jax.ShapeDtypeStruct((9, 4, HID), F32),
        ),
        in_specs=[vmem] * 9,
        out_specs=(vmem,) * 4,
        scratch_shapes=[
            pltpu.VMEM((GROUP, 64, TILE), BF16),
            pltpu.VMEM((blocks, 3, 64, TILE), BF16),
            field, field, field, field, field,
            pltpu.VMEM((rows * 4 + 16, WIDE), F32),
            pltpu.VMEM((rows * 16, WIDE), F32),
            pltpu.VMEM((128, 96), BF16),
            pltpu.VMEM((16, 576), BF16),
            pltpu.VMEM((128, 576), BF16),
            pltpu.VMEM((128, 576), BF16),
            pltpu.VMEM((16, 576), BF16),
            pltpu.VMEM((128, 96), BF16),
            pltpu.VMEM((128, 640), F32),
            pltpu.VMEM((64, 512), F32),
            narrow, narrow, wide, wide, wide, wide,
            pltpu.VMEM((128, 128), F32),
            pltpu.VMEM((8, 128), F32),
            pltpu.VMEM((15, 8, 128), F32),
            pltpu.VMEM((128, 128), F32),
            pltpu.VMEM((GROUP, 16, TILE), F32),
            pltpu.VMEM((GROUP, 16, TILE), F32),
            pltpu.SemaphoreType.DMA((sends,)),
            pltpu.SemaphoreType.DMA((blocks, 3)),
            pltpu.SemaphoreType.DMA((GROUP,)),
            pltpu.SemaphoreType.DMA((GROUP,)),
            pltpu.SemaphoreType.DMA((15,)),
            pltpu.SemaphoreType.DMA((15,)),
            pltpu.SemaphoreType.DMA((15,)),
            pltpu.SemaphoreType.DMA((15,)),
        ],
        compiler_params=pltpu.CompilerParams(
            collective_id=0, has_side_effects=True, vmem_limit_bytes=48 * 1024 * 1024
        ),
    )(
        tracers, forcing, diffusivity, ocean_mask, wi, wm, wo, sensitivity,
        jnp.asarray(spread_matrix(), BF16),
    )
    if n_lat * n_lon != 16:
        g_in, g_mid, g_out = lax.psum((g_in, g_mid, g_out), ("lon", "lat"))
    return (
        final.transpose(1, 0, 2),
        g_in.reshape(3, 3, 4, HID).transpose(3, 2, 0, 1),
        g_mid.reshape(3, 3, HID, HID).transpose(2, 3, 0, 1),
        g_out.reshape(3, 3, 4, HID).transpose(2, 3, 0, 1),
    )


def solution(mesh):
    field = P("ens", "lat", "lon")
    cells = P("lat", "lon")
    gradient = P("ens", None, None, None)
    return jax.shard_map(
        functools.partial(on_device, mesh.shape["lat"], mesh.shape["lon"]),
        mesh=mesh,
        in_specs=(field, field, cells, cells, P(), P(), P(), field),
        out_specs=(field, gradient, gradient, gradient),
        check_vma=False,
    )
```

```python
import functools
import math

import jax
import jax.numpy as jnp
from jax import lax
from jax.experimental import pallas as pl
from jax.experimental.pallas import tpu as pltpu
from jax.sharding import PartitionSpec as P

GAIN = 0.5
VMEM_GRANT = 63 * 1024 * 1024 + 512 * 1024
MESH = pl.DeviceIdType.MESH
F32 = jnp.float32
BF16 = jnp.bfloat16
TILE = 128
WIDE = 256
HID = 32
DEEP = 3 * HID
GROUP = 4
OWN_ROWS = 16


def dot(a, b):
    return jnp.dot(a, b, preferred_element_type=F32)


def dot_nt(a, b):
    return lax.dot_general(a, b, (((1,), (1,)), ((), ())), preferred_element_type=F32)


def left_of(v):
    return pltpu.roll(v, 1, 1)


def right_of(v):
    return pltpu.roll(v, WIDE - 1, 1)


def spread_matrix():
    i = lax.broadcasted_iota(jnp.int32, (80, 64), 0)
    k = lax.broadcasted_iota(jnp.int32, (80, 64), 1)
    array, r, c = i // 16, (i % 16) // 4, i % 4
    at = jnp.where(array < 3, array * 16 + c * 4 + r, 36 + array * 4 + r)
    return (k == at).astype(F32).astype(BF16)


def kernel(
    n_lat, n_lon, halo, scale,
    tr_hbm, fo_hbm, ka_hbm, ma_hbm, wi_hbm, wm_hbm, wo_hbm, se_hbm,
    final_hbm, gin_hbm, gmid_hbm, gout_hbm,
    final_ref, gin_ref, gmid_ref, gout_ref, out_sem,
    tr_ref, fo_ref, ka_ref, ma_ref, wi_ref, wm_ref, wo_ref, se_ref, in_sem,
    pk, rbuf, st, fo, se, ka, ma, lap, sixteen,
    t_if, t_ib, t_mf, t_mb, t_of, t_ob, t_tmp, t_wide,
    src, cc, h1, h2, l2, l1, acc, chunk, rs, total, fsrc, fdst,
    x_send, x_recv, f_send, f_recv, rs_send, rs_recv, ag_send, ag_recv,
):
    lat = lax.axis_index("lat")
    lon = lax.axis_index("lon")
    group = lat // GROUP
    j = lat % GROUP
    n_groups = n_lat // GROUP
    blocks = GROUP + 2 * halo
    rows = 4 * blocks
    reduce_here = n_lat * n_lon == 16

    loads = [
        pltpu.make_async_copy(there, here, in_sem.at[i])
        for i, (there, here) in enumerate(
            (
                (tr_hbm, tr_ref), (fo_hbm, fo_ref), (se_hbm, se_ref), (ka_hbm, ka_ref),
                (ma_hbm, ma_ref), (wi_hbm, wi_ref), (wm_hbm, wm_ref), (wo_hbm, wo_ref),
            )
        )
    ]
    for load in loads:
        load.start()

    barrier = pltpu.get_barrier_semaphore()
    if reduce_here:
        peers = [(dl, dz) for dz in range(n_lon) for dl in range(n_lat) if (dl, dz) != (0, 0)]
        peer_ids = [((lat + dl) % n_lat, (lon + dz) % n_lon) for dl, dz in peers]
    else:
        peer_ids = []
        for dg in (-1, 0, 1):
            for dj in range(GROUP):
                for dz in (-1, 0, 1):
                    if (dg, dj, dz) != (0, 0, 0):
                        other = (group + dg + n_groups) % n_groups
                        peer_ids.append((other * GROUP + (j + dj) % GROUP, (lon + dz + n_lon) % n_lon))
    for pl_lat, pl_lon in peer_ids:
        pl.semaphore_signal(
            barrier, inc=1, device_id={"lat": pl_lat, "lon": pl_lon}, device_id_type=MESH
        )

    spread = spread_matrix()
    for load in loads[:5]:
        load.wait()
    pieces = [tr_ref[c] for c in range(4)] + [fo_ref[c] for c in range(4)] + [se_ref[c] for c in range(4)]
    pieces += [ka_ref[...], ma_ref[...].astype(F32)]
    for i, piece in enumerate(pieces):
        t_wide[i * 4 : i * 4 + 4, :] = piece
    t_wide[56:64, :] = jnp.zeros((8, 512), F32)
    packed = t_wide[...].astype(BF16)
    for t in range(GROUP):
        pk[t] = packed[:, t * TILE : (t + 1) * TILE]

    pl.semaphore_wait(barrier, len(peer_ids))

    waits = []

    def send(tile, slot, which, sem, to_lat, to_lon, when):
        copy = pltpu.make_async_remote_copy(
            src_ref=pk.at[tile],
            dst_ref=rbuf.at[slot, which],
            send_sem=x_send.at[sem],
            recv_sem=x_recv.at[slot, which],
            device_id={"lat": to_lat, "lon": to_lon},
            device_id_type=MESH,
        )
        if when is None:
            copy.start()
        else:
            pl.when(when)(copy.start)
        waits.append((copy, when))

    def keep(tile, slot, which, when):
        copy = pltpu.make_async_copy(pk.at[tile], rbuf.at[slot, which], x_recv.at[slot, which])
        if when is None:
            copy.start()
        else:
            pl.when(when)(copy.start)

    number = 0
    for dg in (0,) if halo == 0 else (-1, 0, 1):
        gate = None if dg == 0 else (j >= 1 if dg == 1 else j <= 2)
        to_group = ((group + dg + n_groups) % n_groups) * GROUP
        slot = j - 4 * dg + halo
        for s in (1, 2, 3, 0):
            t = (j + s) % GROUP
            own = dg == 0
            if own and s == 0:
                keep(t, slot, 1, None)
            else:
                send(t, slot, 1, number, to_group + t, lon, gate)
            number += 1
            if own and s == 3:
                keep(t, slot, 0, t != 3)
                when = t == 3
            else:
                when = gate
            send(
                t, slot, 0, number, to_group + (t + 1) % GROUP,
                (lon + (t == 3).astype(jnp.int32)) % n_lon, when,
            )
            number += 1
            if own and s == 1:
                keep(t, slot, 2, t != 0)
                when = t == 0
            else:
                when = gate
            send(
                t, slot, 2, number, to_group + (t + 3) % GROUP,
                (lon + n_lon - (t == 0).astype(jnp.int32)) % n_lon, when,
            )
            number += 1

    def banded_wide(parts, out_rows, target):
        t_tmp[...] = jnp.zeros_like(t_tmp)
        strip = jnp.concatenate(parts, axis=1)
        for r in range(4):
            t_tmp[r * out_rows : (r + 1) * out_rows, r * DEEP : r * DEEP + 3 * DEEP] = strip
        target[...] = t_tmp[0 : 4 * out_rows, 0 : 6 * DEEP].astype(BF16)

    def banded_narrow(parts, target):
        t_tmp[0:128, 0:128] = jnp.zeros((128, 128), F32)
        for r in range(4):
            for a in range(3):
                for b in range(3):
                    top = (r + a) * 16 + b * 4
                    t_tmp[top : top + 4, r * HID : (r + 1) * HID] = parts[a * 3 + b]
        target[...] = jnp.transpose(t_tmp[0:128, 0:128])[:, 0:96].astype(BF16)

    for load in loads[5:]:
        load.wait()
    wi = [wi_ref[k].astype(F32) for k in range(9)]
    wm = [wm_ref[k].astype(F32) for k in range(9)]
    wo = [wo_ref[k].astype(F32) for k in range(9)]
    banded_narrow(wi, t_if)
    banded_wide(wm, HID, t_mf)
    banded_wide(wo, 4, t_of)
    banded_narrow(wo[::-1], t_ob)
    banded_wide([jnp.transpose(w) for w in wm[::-1]], HID, t_mb)
    banded_wide(wi[::-1], 4, t_ib)

    for buf in (h1, h2, l2, l1):
        for n in range(2):
            buf[n, 0:DEEP, :] = jnp.zeros((DEEP, WIDE), BF16)
            buf[n, (rows + 1) * DEEP : (rows + 2) * DEEP, :] = jnp.zeros((DEEP, WIDE), BF16)
    for buf in (src, cc):
        for n in range(2):
            buf[n, 0:16, :] = jnp.zeros((16, WIDE), BF16)
            buf[n, (rows + 1) * 16 : (rows + 2) * 16, :] = jnp.zeros((16, WIDE), BF16)
    sixteen[...] = jnp.zeros_like(sixteen)
    lap[...] = jnp.zeros_like(lap)

    def inside(per_row, count, first):
        if halo == 0:
            return None
        at = lax.broadcasted_iota(jnp.int32, (count, WIDE), 0) // per_row + first
        at = at + (group * GROUP - halo) * 4
        return ((at >= 0) & (at < n_lat * 4)).astype(F32)

    def clear(v, per_row, first):
        if halo == 0:
            return v
        return v * inside(per_row, v.shape[0], first)

    lane = lax.broadcasted_iota(jnp.int32, (80, TILE), 1)
    for w in range(blocks):
        for which in range(3):
            pltpu.make_async_copy(pk.at[0], rbuf.at[w, which], x_recv.at[w, which]).wait()
    for w in range(blocks):
        three = jnp.concatenate([rbuf[w, 1], rbuf[w, 0], rbuf[w, 2]], axis=1)
        got = dot(spread, three)
        side = jnp.where(lane < TILE // 2, got[:, 2 * TILE :], got[:, TILE : 2 * TILE])
        both = jnp.concatenate([got[:, 0:TILE], side], axis=1)
        here = slice(w * 16, (w + 1) * 16)
        st[here, :] = clear(both[0:16], 4, 4 * w)
        fo[here, :] = both[16:32]
        se[here, :] = both[32:48]
        ka[here, :] = both[48:64]
        ma[here, :] = clear(both[64:80], 4, 4 * w)

    def put_narrow(target, n, v):
        for b, moved in enumerate((left_of(v), v, right_of(v))):
            for r in range(rows):
                sixteen[r * 16 + b * 4 : r * 16 + b * 4 + 4, :] = moved[r * 4 : r * 4 + 4]
        target[n, 16 : 16 + rows * 16, :] = sixteen[...].astype(BF16)

    def put_wide(target, n, w, v):
        v = clear(v, HID, 4 * w)
        for b, moved in enumerate((left_of(v), v, right_of(v))):
            moved = moved.astype(BF16)
            for r in range(4):
                top = (4 * w + r + 1) * DEEP + b * HID
                target[n, top : top + HID, :] = moved[r * HID : (r + 1) * HID]

    def centre(target, n, w):
        parts = []
        for r in range(4):
            top = (4 * w + r + 1) * DEEP + HID
            parts.append(target[n, top : top + HID, :])
        return jnp.concatenate(parts, axis=0).astype(F32)

    def narrow_window(target, n, w):
        return target[n, w * 64 : w * 64 + 96, :]

    def wide_window(target, n, w):
        return target[n, 4 * w * DEEP : 4 * w * DEEP + 6 * DEEP, :]

    def laplace(v):
        lap[8 : 8 + rows * 4, :] = v
        up = lap[4 : 4 + rows * 4, :]
        down = lap[12 : 12 + rows * 4, :]
        return up + down + left_of(v) + right_of(v) - 4.0 * v

    def forward(n, state):
        put_narrow(src, n, state)
        for w in range(blocks):
            put_wide(h1, n, w, jnp.tanh(dot(t_if[...], narrow_window(src, n, w))))
        for w in range(blocks):
            put_wide(h2, n, w, jnp.tanh(dot(t_mf[...], wide_window(h1, n, w))))
        closure = jnp.concatenate(
            [dot(t_of[...], wide_window(h2, n, w)) for w in range(blocks)], axis=0
        )
        return ma[...] * (state + ka[...] * laplace(state) + GAIN * closure + fo[...])

    def strip_wide(target, n):
        parts = []
        for s in range(OWN_ROWS + 2):
            top = (4 * halo + s) * DEEP
            parts.append(target[n, top : top + DEEP, 0:TILE])
        return jnp.concatenate(parts, axis=1)

    def strip_narrow(target, n):
        parts = []
        for s in range(OWN_ROWS + 2):
            top = (4 * halo + s) * 16
            parts.append(target[n, top : top + 16, 0:TILE])
        return jnp.concatenate(parts, axis=1)

    def strip_shifted(read, height):
        zero = jnp.zeros((height, TILE), BF16)
        cells = [read(r) for r in range(OWN_ROWS)]
        return jnp.concatenate(
            [jnp.concatenate([zero] * a + cells + [zero] * (2 - a), axis=1) for a in range(3)],
            axis=0,
        )

    def read_wide(target, n):
        def read(r):
            top = (4 * halo + r + 1) * DEEP + HID
            return target[n, top : top + HID, 0:TILE]

        return read

    def read_narrow(target, n):
        def read(r):
            top = (4 * halo + r + 1) * 16
            return target[n, top : top + 16, 0:TILE]

        return read

    def backward(n, masked, need_state):
        put_narrow(cc, n, GAIN * masked)
        grad_out = dot_nt(strip_shifted(read_narrow(cc, n), 16), strip_wide(h2, n))
        for w in range(blocks):
            slope = 1.0 - jnp.square(centre(h2, n, w))
            put_wide(l2, n, w, dot(t_ob[...], narrow_window(cc, n, w)) * slope)
        grad_mid = dot_nt(strip_shifted(read_wide(l2, n), HID), strip_wide(h1, n))
        for w in range(blocks):
            slope = 1.0 - jnp.square(centre(h1, n, w))
            put_wide(l1, n, w, dot(t_mb[...], wide_window(l2, n, w)) * slope)
        grad_in = dot_nt(strip_narrow(src, n), strip_shifted(read_wide(l1, n), HID))
        earlier = None
        if need_state:
            through = jnp.concatenate(
                [dot(t_ib[...], wide_window(l1, n, w)) for w in range(blocks)], axis=0
            )
            earlier = masked + laplace(ka[...] * masked) + through
        return earlier, (grad_in, grad_mid, grad_out)

    state = forward(0, st[...])
    final = forward(1, state)
    for i in range(GROUP):
        top = (halo + i) * 16
        fsrc[i] = final[top : top + 16, 0:TILE]
    for s in (1, 2, 3):
        i = (j + s) % GROUP
        copy = pltpu.make_async_remote_copy(
            src_ref=fsrc.at[i],
            dst_ref=fdst.at[j],
            send_sem=f_send.at[s],
            recv_sem=f_recv.at[j],
            device_id={"lat": group * GROUP + i, "lon": lon},
            device_id_type=MESH,
        )
        copy.start()
        waits.append((copy, None))
    pltpu.make_async_copy(fsrc.at[j], fdst.at[j], f_recv.at[j]).start()

    adjoint, late = backward(1, ma[...] * se[...], True)
    _, early = backward(0, ma[...] * adjoint, False)

    g_in, g_mid, g_out = (a + b for a, b in zip(late, early))
    acc[...] = jnp.zeros_like(acc)
    acc[0:96, 0:96] = g_mid * scale
    for a in range(3):
        acc[96 + a * 4 : 100 + a * 4, 0:96] = g_out[a * 16 + 4 : a * 16 + 8] * scale
    acc[108:120, 0:96] = g_in[0:12] * scale

    if reduce_here:
        rank = lon * n_lat + lat
        sums = []
        for o, (to_lat, to_lon) in enumerate(peer_ids):
            other = to_lon * n_lat + to_lat
            copy = pltpu.make_async_remote_copy(
                src_ref=acc.at[pl.ds(pl.multiple_of(other * 8, 8), 8)],
                dst_ref=rs.at[o],
                send_sem=rs_send.at[o],
                recv_sem=rs_recv.at[o],
                device_id={"lat": to_lat, "lon": to_lon},
                device_id_type=MESH,
            )
            copy.start()
            waits.append((copy, None))
            sums.append(copy)
        mine = pl.ds(pl.multiple_of(rank * 8, 8), 8)
        whole = acc[mine, :]
        for o, copy in enumerate(sums):
            copy.wait_recv()
            whole = whole + rs[o]
        chunk[...] = whole
        total[mine, :] = whole
        gathered = []
        for o, (to_lat, to_lon) in enumerate(peer_ids):
            copy = pltpu.make_async_remote_copy(
                src_ref=chunk,
                dst_ref=total.at[mine],
                send_sem=ag_send.at[o],
                recv_sem=ag_recv.at[o],
                device_id={"lat": to_lat, "lon": to_lon},
                device_id_type=MESH,
            )
            copy.start()
            waits.append((copy, None))
            gathered.append(copy)

    for i in range(GROUP):
        pltpu.make_async_copy(fsrc.at[0], fdst.at[i], f_recv.at[i]).wait()
    for i in range(GROUP):
        for r in range(4):
            final_ref[:, r, i * TILE : (i + 1) * TILE] = fdst[i, r * 4 : r * 4 + 4, :]
    stores = [pltpu.make_async_copy(final_ref, final_hbm, out_sem.at[0])]
    stores[0].start()

    if reduce_here:
        for copy in gathered:
            copy.wait_recv()
        result = total[...]
    else:
        result = acc[...]
    for a in range(3):
        for b in range(3):
            k = a * 3 + b
            side = slice(b * HID, (b + 1) * HID)
            gmid_ref[k] = result[a * HID : (a + 1) * HID, side]
            gout_ref[k] = result[96 + a * 4 : 100 + a * 4, side]
            gin_ref[k] = result[108 + b * 4 : 112 + b * 4, a * HID : (a + 1) * HID]
    for i, (here, there) in enumerate(
        ((gin_ref, gin_hbm), (gmid_ref, gmid_hbm), (gout_ref, gout_hbm))
    ):
        stores.append(pltpu.make_async_copy(here, there, out_sem.at[i + 1]))
        stores[-1].start()
    for copy, when in waits:
        if when is None:
            copy.wait_send()
        else:
            pl.when(when)(copy.wait_send)
    for store in stores:
        store.wait()


def hand_on(*refs):
    sem = refs[-1]
    copies = [pltpu.make_async_copy(refs[i], refs[i + 4], sem.at[i]) for i in range(4)]
    for copy in copies:
        copy.start()
    for copy in copies:
        copy.wait()


def on_device(
    n_lat, n_lon,
    tracers, forcing, diffusivity, ocean_mask, weight_in, weight_mid, weight_out, sensitivity,
):
    halo = 0 if n_lat == GROUP else 3
    blocks = GROUP + 2 * halo
    rows = 4 * blocks
    scale = 1.0 / math.sqrt(tracers.shape[1] * n_lat * tracers.shape[2] * n_lon)
    sends = 12 if halo == 0 else 36
    wi = weight_in.transpose(2, 3, 1, 0).reshape(9, 4, HID)
    wm = weight_mid.transpose(2, 3, 0, 1).reshape(9, HID, HID)
    wo = weight_out.transpose(2, 3, 0, 1).reshape(9, 4, HID)
    field = pltpu.VMEM((rows * 4, WIDE), F32)
    wide = pltpu.VMEM((2, (rows + 2) * DEEP, WIDE), BF16)
    narrow = pltpu.VMEM((2, (rows + 2) * 16, WIDE), BF16)
    hbm = pl.BlockSpec(memory_space=pltpu.HBM)
    outs = (
        jax.ShapeDtypeStruct((4, 4, 512), F32),
        jax.ShapeDtypeStruct((9, 4, HID), F32),
        jax.ShapeDtypeStruct((9, HID, HID), F32),
        jax.ShapeDtypeStruct((9, 4, HID), F32),
    )
    final, g_in, g_mid, g_out = pl.pallas_call(
        functools.partial(kernel, n_lat, n_lon, halo, scale),
        out_shape=outs,
        in_specs=[hbm] * 8,
        out_specs=(hbm,) * 4,
        scratch_shapes=[pltpu.VMEM(o.shape, F32) for o in outs]
        + [
            pltpu.SemaphoreType.DMA((4,)),
            pltpu.VMEM((4, 4, 512), F32),
            pltpu.VMEM((4, 4, 512), F32),
            pltpu.VMEM((4, 512), F32),
            pltpu.VMEM((4, 512), jnp.int32),
            pltpu.VMEM((9, 4, HID), BF16),
            pltpu.VMEM((9, HID, HID), BF16),
            pltpu.VMEM((9, 4, HID), BF16),
            pltpu.VMEM((4, 4, 512), F32),
            pltpu.SemaphoreType.DMA((8,)),
            pltpu.VMEM((GROUP, 64, TILE), BF16),
            pltpu.VMEM((blocks, 3, 64, TILE), BF16),
            field, field, field, field, field,
            pltpu.VMEM((rows * 4 + 16, WIDE), F32),
            pltpu.VMEM((rows * 16, WIDE), F32),
            pltpu.VMEM((128, 96), BF16),
            pltpu.VMEM((16, 576), BF16),
            pltpu.VMEM((128, 576), BF16),
            pltpu.VMEM((128, 576), BF16),
            pltpu.VMEM((16, 576), BF16),
            pltpu.VMEM((128, 96), BF16),
            pltpu.VMEM((128, 640), F32),
            pltpu.VMEM((64, 512), F32),
            narrow, narrow, wide, wide, wide, wide,
            pltpu.VMEM((128, 128), F32),
            pltpu.VMEM((8, 128), F32),
            pltpu.VMEM((15, 8, 128), F32),
            pltpu.VMEM((128, 128), F32),
            pltpu.VMEM((GROUP, 16, TILE), F32),
            pltpu.VMEM((GROUP, 16, TILE), F32),
            pltpu.SemaphoreType.DMA((sends,)),
            pltpu.SemaphoreType.DMA((blocks, 3)),
            pltpu.SemaphoreType.DMA((GROUP,)),
            pltpu.SemaphoreType.DMA((GROUP,)),
            pltpu.SemaphoreType.DMA((15,)),
            pltpu.SemaphoreType.DMA((15,)),
            pltpu.SemaphoreType.DMA((15,)),
            pltpu.SemaphoreType.DMA((15,)),
        ],
        compiler_params=pltpu.CompilerParams(
            collective_id=0, has_side_effects=True, vmem_limit_bytes=VMEM_GRANT
        ),
    )(tracers, forcing, diffusivity, ocean_mask, wi, wm, wo, sensitivity)
    if n_lat * n_lon != 16:
        g_in, g_mid, g_out = lax.psum((g_in, g_mid, g_out), ("lon", "lat"))
    final, g_in, g_mid, g_out = pl.pallas_call(
        hand_on,
        out_shape=outs,
        in_specs=[hbm] * 4,
        out_specs=(hbm,) * 4,
        scratch_shapes=[pltpu.SemaphoreType.DMA((4,))],
        compiler_params=pltpu.CompilerParams(vmem_limit_bytes=VMEM_GRANT),
    )(final, g_in, g_mid, g_out)
    return (
        final,
        g_in.reshape(3, 3, 4, HID).transpose(3, 2, 0, 1),
        g_mid.reshape(3, 3, HID, HID).transpose(2, 3, 0, 1),
        g_out.reshape(3, 3, 4, HID).transpose(2, 3, 0, 1),
    )


def solution(mesh):
    field = P("ens", "lat", "lon")
    cells = P("lat", "lon")
    gradient = P("ens", None, None, None)
    return jax.shard_map(
        functools.partial(on_device, mesh.shape["lat"], mesh.shape["lon"]),
        mesh=mesh,
        in_specs=(field, field, cells, cells, P(), P(), P(), field),
        out_specs=(field, gradient, gradient, gradient),
        check_vma=False,
    )
```

```python
import functools
import math

import jax
import jax.numpy as jnp
from jax import lax
from jax.experimental import pallas as pl
from jax.experimental.pallas import tpu as pltpu
from jax.sharding import PartitionSpec as P

GAIN = 0.5
VMEM_GRANT = 63 * 1024 * 1024 + 512 * 1024
MESH = pl.DeviceIdType.MESH
F32 = jnp.float32
BF16 = jnp.bfloat16
TILE = 128
WIDE = 256
HID = 32
DEEP = 3 * HID
GROUP = 4
OWN_ROWS = 16


def dot(a, b):
    return jnp.dot(a, b, preferred_element_type=F32)


def dot_nt(a, b):
    return lax.dot_general(a, b, (((1,), (1,)), ((), ())), preferred_element_type=F32)


def left_of(v):
    return pltpu.roll(v, 1, 1)


def right_of(v):
    return pltpu.roll(v, WIDE - 1, 1)


def spread_matrix():
    i = lax.broadcasted_iota(jnp.int32, (80, 64), 0)
    k = lax.broadcasted_iota(jnp.int32, (80, 64), 1)
    array, r, c = i // 16, (i % 16) // 4, i % 4
    at = jnp.where(array < 3, array * 16 + c * 4 + r, 36 + array * 4 + r)
    return (k == at).astype(F32).astype(BF16)


def kernel(
    n_lat, n_lon, halo, scale,
    tr_hbm, fo_hbm, ka_hbm, ma_hbm, wi_hbm, wm_hbm, wo_hbm, se_hbm,
    final_hbm, gin_hbm, gmid_hbm, gout_hbm,
    final_ref, gin_ref, gmid_ref, gout_ref, out_sem,
    tr_ref, fo_ref, ka_ref, ma_ref, wi_ref, wm_ref, wo_ref, se_ref, in_sem,
    pk, rbuf, st, fo, se, ka, ma, lap, sixteen,
    t_if, t_ib, t_mf, t_mb, t_of, t_ob, t_tmp, t_wide,
    src, cc, h1, h2, l2, l1, acc, chunk, rs, total, fsrc, fdst,
    x_send, x_recv, f_send, f_recv, rs_send, rs_recv, ag_send, ag_recv,
):
    lat = lax.axis_index("lat")
    lon = lax.axis_index("lon")
    group = lat // GROUP
    j = lat % GROUP
    n_groups = n_lat // GROUP
    blocks = GROUP + 2 * halo
    rows = 4 * blocks
    reduce_here = n_lat * n_lon == 16

    loads = [
        pltpu.make_async_copy(there, here, in_sem.at[i])
        for i, (there, here) in enumerate(
            (
                (tr_hbm, tr_ref), (fo_hbm, fo_ref), (se_hbm, se_ref), (ka_hbm, ka_ref),
                (ma_hbm, ma_ref), (wi_hbm, wi_ref), (wm_hbm, wm_ref), (wo_hbm, wo_ref),
            )
        )
    ]
    for load in loads:
        load.start()

    barrier = pltpu.get_barrier_semaphore()
    if reduce_here:
        peers = [(dl, dz) for dz in range(n_lon) for dl in range(n_lat) if (dl, dz) != (0, 0)]
        peer_ids = [((lat + dl) % n_lat, (lon + dz) % n_lon) for dl, dz in peers]
    else:
        peer_ids = []
        for dg in (-1, 0, 1):
            for dj in range(GROUP):
                for dz in (-1, 0, 1):
                    if (dg, dj, dz) != (0, 0, 0):
                        other = (group + dg + n_groups) % n_groups
                        peer_ids.append((other * GROUP + (j + dj) % GROUP, (lon + dz + n_lon) % n_lon))
    for pl_lat, pl_lon in peer_ids:
        pl.semaphore_signal(
            barrier, inc=1, device_id={"lat": pl_lat, "lon": pl_lon}, device_id_type=MESH
        )

    spread = spread_matrix()
    for load in loads[:5]:
        load.wait()
    pieces = [tr_ref[c] for c in range(4)] + [fo_ref[c] for c in range(4)] + [se_ref[c] for c in range(4)]
    pieces += [ka_ref[...], ma_ref[...].astype(F32)]
    for i, piece in enumerate(pieces):
        t_wide[i * 4 : i * 4 + 4, :] = piece
    t_wide[56:64, :] = jnp.zeros((8, 512), F32)
    packed = t_wide[...].astype(BF16)
    for t in range(GROUP):
        pk[t] = packed[:, t * TILE : (t + 1) * TILE]

    pl.semaphore_wait(barrier, len(peer_ids))

    waits = []

    def send(tile, slot, which, sem, to_lat, to_lon, when):
        copy = pltpu.make_async_remote_copy(
            src_ref=pk.at[tile],
            dst_ref=rbuf.at[slot, which],
            send_sem=x_send.at[sem],
            recv_sem=x_recv.at[slot, which],
            device_id={"lat": to_lat, "lon": to_lon},
            device_id_type=MESH,
        )
        if when is None:
            copy.start()
        else:
            pl.when(when)(copy.start)
        waits.append((copy, when))

    def keep(tile, slot, which, when):
        copy = pltpu.make_async_copy(pk.at[tile], rbuf.at[slot, which], x_recv.at[slot, which])
        if when is None:
            copy.start()
        else:
            pl.when(when)(copy.start)

    number = 0
    for dg in (0,) if halo == 0 else (-1, 0, 1):
        gate = None if dg == 0 else (j >= 1 if dg == 1 else j <= 2)
        to_group = ((group + dg + n_groups) % n_groups) * GROUP
        slot = j - 4 * dg + halo
        for s in (1, 2, 3, 0):
            t = (j + s) % GROUP
            own = dg == 0
            if own and s == 0:
                keep(t, slot, 1, None)
            else:
                send(t, slot, 1, number, to_group + t, lon, gate)
            number += 1
            if own and s == 3:
                keep(t, slot, 0, t != 3)
                when = t == 3
            else:
                when = gate
            send(
                t, slot, 0, number, to_group + (t + 1) % GROUP,
                (lon + (t == 3).astype(jnp.int32)) % n_lon, when,
            )
            number += 1
            if own and s == 1:
                keep(t, slot, 2, t != 0)
                when = t == 0
            else:
                when = gate
            send(
                t, slot, 2, number, to_group + (t + 3) % GROUP,
                (lon + n_lon - (t == 0).astype(jnp.int32)) % n_lon, when,
            )
            number += 1

    def banded_wide(parts, out_rows, target):
        t_tmp[...] = jnp.zeros_like(t_tmp)
        strip = jnp.concatenate(parts, axis=1)
        for r in range(4):
            t_tmp[r * out_rows : (r + 1) * out_rows, r * DEEP : r * DEEP + 3 * DEEP] = strip
        target[...] = t_tmp[0 : 4 * out_rows, 0 : 6 * DEEP].astype(BF16)

    def banded_narrow(parts, target):
        t_tmp[0:128, 0:128] = jnp.zeros((128, 128), F32)
        for r in range(4):
            for a in range(3):
                for b in range(3):
                    top = (r + a) * 16 + b * 4
                    t_tmp[top : top + 4, r * HID : (r + 1) * HID] = parts[a * 3 + b]
        target[...] = jnp.transpose(t_tmp[0:128, 0:128])[:, 0:96].astype(BF16)

    for load in loads[5:]:
        load.wait()
    wi = [wi_ref[k].astype(F32) for k in range(9)]
    wm = [wm_ref[k].astype(F32) for k in range(9)]
    wo = [wo_ref[k].astype(F32) for k in range(9)]
    banded_narrow(wi, t_if)
    banded_wide(wm, HID, t_mf)
    banded_wide(wo, 4, t_of)
    banded_narrow(wo[::-1], t_ob)
    banded_wide([jnp.transpose(w) for w in wm[::-1]], HID, t_mb)
    banded_wide(wi[::-1], 4, t_ib)

    for buf in (h1, h2, l2, l1):
        for n in range(2):
            buf[n, 0:DEEP, :] = jnp.zeros((DEEP, WIDE), BF16)
            buf[n, (rows + 1) * DEEP : (rows + 2) * DEEP, :] = jnp.zeros((DEEP, WIDE), BF16)
    for buf in (src, cc):
        for n in range(2):
            buf[n, 0:16, :] = jnp.zeros((16, WIDE), BF16)
            buf[n, (rows + 1) * 16 : (rows + 2) * 16, :] = jnp.zeros((16, WIDE), BF16)
    sixteen[...] = jnp.zeros_like(sixteen)
    lap[...] = jnp.zeros_like(lap)

    def inside(per_row, count, first):
        if halo == 0:
            return None
        at = lax.broadcasted_iota(jnp.int32, (count, WIDE), 0) // per_row + first
        at = at + (group * GROUP - halo) * 4
        return ((at >= 0) & (at < n_lat * 4)).astype(F32)

    def clear(v, per_row, first):
        if halo == 0:
            return v
        return v * inside(per_row, v.shape[0], first)

    lane = lax.broadcasted_iota(jnp.int32, (80, TILE), 1)
    for w in range(blocks):
        for which in range(3):
            pltpu.make_async_copy(pk.at[0], rbuf.at[w, which], x_recv.at[w, which]).wait()
    for w in range(blocks):
        three = jnp.concatenate([rbuf[w, 1], rbuf[w, 0], rbuf[w, 2]], axis=1)
        got = dot(spread, three)
        side = jnp.where(lane < TILE // 2, got[:, 2 * TILE :], got[:, TILE : 2 * TILE])
        both = jnp.concatenate([got[:, 0:TILE], side], axis=1)
        here = slice(w * 16, (w + 1) * 16)
        st[here, :] = clear(both[0:16], 4, 4 * w)
        fo[here, :] = both[16:32]
        se[here, :] = both[32:48]
        ka[here, :] = both[48:64]
        ma[here, :] = clear(both[64:80], 4, 4 * w)

    def put_narrow(target, n, v):
        for b, moved in enumerate((left_of(v), v, right_of(v))):
            for r in range(rows):
                sixteen[r * 16 + b * 4 : r * 16 + b * 4 + 4, :] = moved[r * 4 : r * 4 + 4]
        target[n, 16 : 16 + rows * 16, :] = sixteen[...].astype(BF16)

    def put_wide(target, n, w, v):
        v = clear(v, HID, 4 * w)
        for b, moved in enumerate((left_of(v), v, right_of(v))):
            moved = moved.astype(BF16)
            for r in range(4):
                top = (4 * w + r + 1) * DEEP + b * HID
                target[n, top : top + HID, :] = moved[r * HID : (r + 1) * HID]

    def centre(target, n, w):
        parts = []
        for r in range(4):
            top = (4 * w + r + 1) * DEEP + HID
            parts.append(target[n, top : top + HID, :])
        return jnp.concatenate(parts, axis=0).astype(F32)

    def narrow_window(target, n, w):
        return target[n, w * 64 : w * 64 + 96, :]

    def wide_window(target, n, w):
        return target[n, 4 * w * DEEP : 4 * w * DEEP + 6 * DEEP, :]

    def laplace(v):
        lap[8 : 8 + rows * 4, :] = v
        up = lap[4 : 4 + rows * 4, :]
        down = lap[12 : 12 + rows * 4, :]
        return up + down + left_of(v) + right_of(v) - 4.0 * v

    def forward(n, state):
        put_narrow(src, n, state)
        for w in range(blocks):
            put_wide(h1, n, w, jnp.tanh(dot(t_if[...], narrow_window(src, n, w))))
        for w in range(blocks):
            put_wide(h2, n, w, jnp.tanh(dot(t_mf[...], wide_window(h1, n, w))))
        closure = jnp.concatenate(
            [dot(t_of[...], wide_window(h2, n, w)) for w in range(blocks)], axis=0
        )
        return ma[...] * (state + ka[...] * laplace(state) + GAIN * closure + fo[...])

    def strip_wide(target, n):
        parts = []
        for s in range(OWN_ROWS + 2):
            top = (4 * halo + s) * DEEP
            parts.append(target[n, top : top + DEEP, 0:TILE])
        return jnp.concatenate(parts, axis=1)

    def strip_narrow(target, n):
        parts = []
        for s in range(OWN_ROWS + 2):
            top = (4 * halo + s) * 16
            parts.append(target[n, top : top + 16, 0:TILE])
        return jnp.concatenate(parts, axis=1)

    def strip_shifted(read, height):
        zero = jnp.zeros((height, TILE), BF16)
        cells = [read(r) for r in range(OWN_ROWS)]
        return jnp.concatenate(
            [jnp.concatenate([zero] * a + cells + [zero] * (2 - a), axis=1) for a in range(3)],
            axis=0,
        )

    def read_wide(target, n):
        def read(r):
            top = (4 * halo + r + 1) * DEEP + HID
            return target[n, top : top + HID, 0:TILE]

        return read

    def read_narrow(target, n):
        def read(r):
            top = (4 * halo + r + 1) * 16
            return target[n, top : top + 16, 0:TILE]

        return read

    def backward(n, masked, need_state):
        put_narrow(cc, n, GAIN * masked)
        grad_out = dot_nt(strip_shifted(read_narrow(cc, n), 16), strip_wide(h2, n))
        for w in range(blocks):
            slope = 1.0 - jnp.square(centre(h2, n, w))
            put_wide(l2, n, w, dot(t_ob[...], narrow_window(cc, n, w)) * slope)
        grad_mid = dot_nt(strip_shifted(read_wide(l2, n), HID), strip_wide(h1, n))
        for w in range(blocks):
            slope = 1.0 - jnp.square(centre(h1, n, w))
            put_wide(l1, n, w, dot(t_mb[...], wide_window(l2, n, w)) * slope)
        grad_in = dot_nt(strip_narrow(src, n), strip_shifted(read_wide(l1, n), HID))
        earlier = None
        if need_state:
            through = jnp.concatenate(
                [dot(t_ib[...], wide_window(l1, n, w)) for w in range(blocks)], axis=0
            )
            earlier = masked + laplace(ka[...] * masked) + through
        return earlier, (grad_in, grad_mid, grad_out)

    state = forward(0, st[...])
    final = forward(1, state)
    for i in range(GROUP):
        top = (halo + i) * 16
        fsrc[i] = final[top : top + 16, 0:TILE]
    for s in (1, 2, 3):
        i = (j + s) % GROUP
        copy = pltpu.make_async_remote_copy(
            src_ref=fsrc.at[i],
            dst_ref=fdst.at[j],
            send_sem=f_send.at[s],
            recv_sem=f_recv.at[j],
            device_id={"lat": group * GROUP + i, "lon": lon},
            device_id_type=MESH,
        )
        copy.start()
        waits.append((copy, None))
    pltpu.make_async_copy(fsrc.at[j], fdst.at[j], f_recv.at[j]).start()

    adjoint, late = backward(1, ma[...] * se[...], True)
    _, early = backward(0, ma[...] * adjoint, False)

    g_in, g_mid, g_out = (a + b for a, b in zip(late, early))
    acc[...] = jnp.zeros_like(acc)
    acc[0:96, 0:96] = g_mid * scale
    for a in range(3):
        acc[96 + a * 4 : 100 + a * 4, 0:96] = g_out[a * 16 + 4 : a * 16 + 8] * scale
    acc[108:120, 0:96] = g_in[0:12] * scale

    if reduce_here:
        rank = lon * n_lat + lat
        sums = []
        for o, (to_lat, to_lon) in enumerate(peer_ids):
            other = to_lon * n_lat + to_lat
            copy = pltpu.make_async_remote_copy(
                src_ref=acc.at[pl.ds(pl.multiple_of(other * 8, 8), 8)],
                dst_ref=rs.at[o],
                send_sem=rs_send.at[o],
                recv_sem=rs_recv.at[o],
                device_id={"lat": to_lat, "lon": to_lon},
                device_id_type=MESH,
            )
            copy.start()
            waits.append((copy, None))
            sums.append(copy)
        mine = pl.ds(pl.multiple_of(rank * 8, 8), 8)
        whole = acc[mine, :]
        for o, copy in enumerate(sums):
            copy.wait_recv()
            whole = whole + rs[o]
        chunk[...] = whole
        total[mine, :] = whole
        gathered = []
        for o, (to_lat, to_lon) in enumerate(peer_ids):
            copy = pltpu.make_async_remote_copy(
                src_ref=chunk,
                dst_ref=total.at[mine],
                send_sem=ag_send.at[o],
                recv_sem=ag_recv.at[o],
                device_id={"lat": to_lat, "lon": to_lon},
                device_id_type=MESH,
            )
            copy.start()
            waits.append((copy, None))
            gathered.append(copy)

    for i in range(GROUP):
        pltpu.make_async_copy(fsrc.at[0], fdst.at[i], f_recv.at[i]).wait()
    for i in range(GROUP):
        for r in range(4):
            final_ref[:, r, i * TILE : (i + 1) * TILE] = fdst[i, r * 4 : r * 4 + 4, :]
    stores = [pltpu.make_async_copy(final_ref, final_hbm, out_sem.at[0])]
    stores[0].start()

    if reduce_here:
        for copy in gathered:
            copy.wait_recv()
        result = total[...]
    else:
        result = acc[...]
    for a in range(3):
        for b in range(3):
            k = a * 3 + b
            side = slice(b * HID, (b + 1) * HID)
            gmid_ref[k] = result[a * HID : (a + 1) * HID, side]
            gout_ref[k] = result[96 + a * 4 : 100 + a * 4, side]
            gin_ref[k] = result[108 + b * 4 : 112 + b * 4, a * HID : (a + 1) * HID]
    for i, (here, there) in enumerate(
        ((gin_ref, gin_hbm), (gmid_ref, gmid_hbm), (gout_ref, gout_hbm))
    ):
        stores.append(pltpu.make_async_copy(here, there, out_sem.at[i + 1]))
        stores[-1].start()
    for copy, when in waits:
        if when is None:
            copy.wait_send()
        else:
            pl.when(when)(copy.wait_send)
    for store in stores:
        store.wait()


def hand_on(*refs):
    there, back, held, sems = refs[:4], refs[4:8], refs[8:12], refs[12]
    reads = [pltpu.make_async_copy(there[i], held[i], sems.at[0, i]) for i in range(4)]
    writes = [pltpu.make_async_copy(held[i], back[i], sems.at[1, i]) for i in range(4)]
    for read in reads:
        read.start()
    for read, write in zip(reads, writes):
        read.wait()
        write.start()
    for write in writes:
        write.wait()


def on_device(
    n_lat, n_lon,
    tracers, forcing, diffusivity, ocean_mask, weight_in, weight_mid, weight_out, sensitivity,
):
    halo = 0 if n_lat == GROUP else 3
    blocks = GROUP + 2 * halo
    rows = 4 * blocks
    scale = 1.0 / math.sqrt(tracers.shape[1] * n_lat * tracers.shape[2] * n_lon)
    sends = 12 if halo == 0 else 36
    wi = weight_in.transpose(2, 3, 1, 0).reshape(9, 4, HID)
    wm = weight_mid.transpose(2, 3, 0, 1).reshape(9, HID, HID)
    wo = weight_out.transpose(2, 3, 0, 1).reshape(9, 4, HID)
    field = pltpu.VMEM((rows * 4, WIDE), F32)
    wide = pltpu.VMEM((2, (rows + 2) * DEEP, WIDE), BF16)
    narrow = pltpu.VMEM((2, (rows + 2) * 16, WIDE), BF16)
    hbm = pl.BlockSpec(memory_space=pltpu.HBM)
    outs = (
        jax.ShapeDtypeStruct((4, 4, 512), F32),
        jax.ShapeDtypeStruct((9, 4, HID), F32),
        jax.ShapeDtypeStruct((9, HID, HID), F32),
        jax.ShapeDtypeStruct((9, 4, HID), F32),
    )
    final, g_in, g_mid, g_out = pl.pallas_call(
        functools.partial(kernel, n_lat, n_lon, halo, scale),
        out_shape=outs,
        in_specs=[hbm] * 8,
        out_specs=(hbm,) * 4,
        scratch_shapes=[pltpu.VMEM(o.shape, F32) for o in outs]
        + [
            pltpu.SemaphoreType.DMA((4,)),
            pltpu.VMEM((4, 4, 512), F32),
            pltpu.VMEM((4, 4, 512), F32),
            pltpu.VMEM((4, 512), F32),
            pltpu.VMEM((4, 512), jnp.int32),
            pltpu.VMEM((9, 4, HID), BF16),
            pltpu.VMEM((9, HID, HID), BF16),
            pltpu.VMEM((9, 4, HID), BF16),
            pltpu.VMEM((4, 4, 512), F32),
            pltpu.SemaphoreType.DMA((8,)),
            pltpu.VMEM((GROUP, 64, TILE), BF16),
            pltpu.VMEM((blocks, 3, 64, TILE), BF16),
            field, field, field, field, field,
            pltpu.VMEM((rows * 4 + 16, WIDE), F32),
            pltpu.VMEM((rows * 16, WIDE), F32),
            pltpu.VMEM((128, 96), BF16),
            pltpu.VMEM((16, 576), BF16),
            pltpu.VMEM((128, 576), BF16),
            pltpu.VMEM((128, 576), BF16),
            pltpu.VMEM((16, 576), BF16),
            pltpu.VMEM((128, 96), BF16),
            pltpu.VMEM((128, 640), F32),
            pltpu.VMEM((64, 512), F32),
            narrow, narrow, wide, wide, wide, wide,
            pltpu.VMEM((128, 128), F32),
            pltpu.VMEM((8, 128), F32),
            pltpu.VMEM((15, 8, 128), F32),
            pltpu.VMEM((128, 128), F32),
            pltpu.VMEM((GROUP, 16, TILE), F32),
            pltpu.VMEM((GROUP, 16, TILE), F32),
            pltpu.SemaphoreType.DMA((sends,)),
            pltpu.SemaphoreType.DMA((blocks, 3)),
            pltpu.SemaphoreType.DMA((GROUP,)),
            pltpu.SemaphoreType.DMA((GROUP,)),
            pltpu.SemaphoreType.DMA((15,)),
            pltpu.SemaphoreType.DMA((15,)),
            pltpu.SemaphoreType.DMA((15,)),
            pltpu.SemaphoreType.DMA((15,)),
        ],
        compiler_params=pltpu.CompilerParams(
            collective_id=0, has_side_effects=True, vmem_limit_bytes=VMEM_GRANT
        ),
    )(tracers, forcing, diffusivity, ocean_mask, wi, wm, wo, sensitivity)
    if n_lat * n_lon != 16:
        g_in, g_mid, g_out = lax.psum((g_in, g_mid, g_out), ("lon", "lat"))
    final, g_in, g_mid, g_out = pl.pallas_call(
        hand_on,
        out_shape=outs,
        in_specs=[hbm] * 4,
        out_specs=(hbm,) * 4,
        scratch_shapes=[pltpu.VMEM(o.shape, F32) for o in outs]
        + [pltpu.SemaphoreType.DMA((2, 4))],
        compiler_params=pltpu.CompilerParams(vmem_limit_bytes=VMEM_GRANT),
    )(final, g_in, g_mid, g_out)
    return (
        final,
        g_in.reshape(3, 3, 4, HID).transpose(3, 2, 0, 1),
        g_mid.reshape(3, 3, HID, HID).transpose(2, 3, 0, 1),
        g_out.reshape(3, 3, 4, HID).transpose(2, 3, 0, 1),
    )


def solution(mesh):
    field = P("ens", "lat", "lon")
    cells = P("lat", "lon")
    gradient = P("ens", None, None, None)
    return jax.shard_map(
        functools.partial(on_device, mesh.shape["lat"], mesh.shape["lon"]),
        mesh=mesh,
        in_specs=(field, field, cells, cells, P(), P(), P(), field),
        out_specs=(field, gradient, gradient, gradient),
        check_vma=False,
    )
```

```python
import functools
import math

import jax
import jax.numpy as jnp
from jax import lax
from jax.experimental import pallas as pl
from jax.experimental.pallas import tpu as pltpu
from jax.sharding import PartitionSpec as P

GAIN = 0.5
VMEM_GRANT = 63 * 1024 * 1024 + 512 * 1024
MESH = pl.DeviceIdType.MESH
F32 = jnp.float32
BF16 = jnp.bfloat16
TILE = 128
WIDE = 256
HID = 32
DEEP = 3 * HID
GROUP = 4
OWN_ROWS = 16


def dot(a, b):
    return jnp.dot(a, b, preferred_element_type=F32)


def dot_nt(a, b):
    return lax.dot_general(a, b, (((1,), (1,)), ((), ())), preferred_element_type=F32)


def left_of(v):
    return pltpu.roll(v, 1, 1)


def right_of(v):
    return pltpu.roll(v, WIDE - 1, 1)


def spread_matrix():
    i = lax.broadcasted_iota(jnp.int32, (80, 64), 0)
    k = lax.broadcasted_iota(jnp.int32, (80, 64), 1)
    array, r, c = i // 16, (i % 16) // 4, i % 4
    at = jnp.where(array < 3, array * 16 + c * 4 + r, 36 + array * 4 + r)
    return (k == at).astype(F32).astype(BF16)


def kernel(
    n_lat, n_lon, halo, scale,
    tr_hbm, fo_hbm, ka_hbm, ma_hbm, wi_hbm, wm_hbm, wo_hbm, se_hbm,
    final_hbm, gin_hbm, gmid_hbm, gout_hbm,
    final_ref, gin_ref, gmid_ref, gout_ref, out_sem,
    tr_ref, fo_ref, ka_ref, ma_ref, wi_ref, wm_ref, wo_ref, se_ref, in_sem,
    pk, pe, rbuf, ebuf, st, fo, se, ka, ma, lap, sixteen,
    t_if, t_ib, t_mf, t_mb, t_of, t_ob, t_tmp, t_wide,
    src, cc, h1, h2, l2, l1, acc, chunk, rs, total, fsrc, fdst,
    x_send, x_recv, f_send, f_recv, rs_send, rs_recv, ag_send, ag_recv,
):
    lat = lax.axis_index("lat")
    lon = lax.axis_index("lon")
    group = lat // GROUP
    j = lat % GROUP
    n_groups = n_lat // GROUP
    blocks = GROUP + 2 * halo
    rows = 4 * blocks
    reduce_here = n_lat * n_lon == 16

    loads = [
        pltpu.make_async_copy(there, here, in_sem.at[i])
        for i, (there, here) in enumerate(
            (
                (tr_hbm, tr_ref), (fo_hbm, fo_ref), (se_hbm, se_ref), (ka_hbm, ka_ref),
                (ma_hbm, ma_ref), (wi_hbm, wi_ref), (wm_hbm, wm_ref), (wo_hbm, wo_ref),
            )
        )
    ]
    for load in loads:
        load.start()

    barrier = pltpu.get_barrier_semaphore()
    if reduce_here:
        peers = [(dl, dz) for dz in range(n_lon) for dl in range(n_lat) if (dl, dz) != (0, 0)]
        peer_ids = [((lat + dl) % n_lat, (lon + dz) % n_lon) for dl, dz in peers]
    else:
        peer_ids = []
        for dg in (-1, 0, 1):
            for dj in range(GROUP):
                for dz in (-1, 0, 1):
                    if (dg, dj, dz) != (0, 0, 0):
                        other = (group + dg + n_groups) % n_groups
                        peer_ids.append((other * GROUP + (j + dj) % GROUP, (lon + dz + n_lon) % n_lon))
    for pl_lat, pl_lon in peer_ids:
        pl.semaphore_signal(
            barrier, inc=1, device_id={"lat": pl_lat, "lon": pl_lon}, device_id_type=MESH
        )

    spread = spread_matrix()
    for load in loads[:5]:
        load.wait()
    pieces = [tr_ref[c] for c in range(4)] + [fo_ref[c] for c in range(4)] + [se_ref[c] for c in range(4)]
    pieces += [ka_ref[...], ma_ref[...].astype(F32)]
    for i, piece in enumerate(pieces):
        t_wide[i * 4 : i * 4 + 4, :] = piece
    t_wide[56:64, :] = jnp.zeros((8, 512), F32)
    packed = t_wide[...].astype(BF16)
    low = lax.broadcasted_iota(jnp.int32, (32, TILE), 1) < TILE // 2
    for t in range(GROUP):
        pk[t] = packed[:, t * TILE : (t + 1) * TILE]
        upper = t_wide[0:32, t * TILE : (t + 1) * TILE]
        lower = pltpu.roll(t_wide[32:64, t * TILE : (t + 1) * TILE], TILE // 2, 1)
        pe[t, 0] = jnp.where(low, lower, upper).astype(BF16)
        pe[t, 1] = jnp.where(low, upper, lower).astype(BF16)

    pl.semaphore_wait(barrier, len(peer_ids))

    waits = []

    def ends(tile, slot, which):
        if which == 1:
            return pk.at[tile], rbuf.at[slot]
        return pe.at[tile, which // 2], ebuf.at[slot, which // 2]

    def send(tile, slot, which, sem, to_lat, to_lon, when):
        source, target = ends(tile, slot, which)
        copy = pltpu.make_async_remote_copy(
            src_ref=source,
            dst_ref=target,
            send_sem=x_send.at[sem],
            recv_sem=x_recv.at[slot, which],
            device_id={"lat": to_lat, "lon": to_lon},
            device_id_type=MESH,
        )
        if when is None:
            copy.start()
        else:
            pl.when(when)(copy.start)
        waits.append((copy, when))

    def keep(tile, slot, which, when):
        copy = pltpu.make_async_copy(*ends(tile, slot, which), x_recv.at[slot, which])
        if when is None:
            copy.start()
        else:
            pl.when(when)(copy.start)

    number = 0
    for dg in (0,) if halo == 0 else (-1, 0, 1):
        gate = None if dg == 0 else (j >= 1 if dg == 1 else j <= 2)
        to_group = ((group + dg + n_groups) % n_groups) * GROUP
        slot = j - 4 * dg + halo
        for s in (1, 2, 3, 0):
            t = (j + s) % GROUP
            own = dg == 0
            if own and s == 0:
                keep(t, slot, 1, None)
            else:
                send(t, slot, 1, number, to_group + t, lon, gate)
            number += 1
            if own and s == 3:
                keep(t, slot, 0, t != 3)
                when = t == 3
            else:
                when = gate
            send(
                t, slot, 0, number, to_group + (t + 1) % GROUP,
                (lon + (t == 3).astype(jnp.int32)) % n_lon, when,
            )
            number += 1
            if own and s == 1:
                keep(t, slot, 2, t != 0)
                when = t == 0
            else:
                when = gate
            send(
                t, slot, 2, number, to_group + (t + 3) % GROUP,
                (lon + n_lon - (t == 0).astype(jnp.int32)) % n_lon, when,
            )
            number += 1

    def banded_wide(parts, out_rows, target):
        t_tmp[...] = jnp.zeros_like(t_tmp)
        strip = jnp.concatenate(parts, axis=1)
        for r in range(4):
            t_tmp[r * out_rows : (r + 1) * out_rows, r * DEEP : r * DEEP + 3 * DEEP] = strip
        target[...] = t_tmp[0 : 4 * out_rows, 0 : 6 * DEEP].astype(BF16)

    def banded_narrow(parts, target):
        t_tmp[0:128, 0:128] = jnp.zeros((128, 128), F32)
        for r in range(4):
            for a in range(3):
                for b in range(3):
                    top = (r + a) * 16 + b * 4
                    t_tmp[top : top + 4, r * HID : (r + 1) * HID] = parts[a * 3 + b]
        target[...] = jnp.transpose(t_tmp[0:128, 0:128])[:, 0:96].astype(BF16)

    for load in loads[5:]:
        load.wait()
    wi = [wi_ref[k].astype(F32) for k in range(9)]
    wm = [wm_ref[k].astype(F32) for k in range(9)]
    wo = [wo_ref[k].astype(F32) for k in range(9)]
    banded_narrow(wi, t_if)
    banded_wide(wm, HID, t_mf)
    banded_wide(wo, 4, t_of)
    banded_narrow(wo[::-1], t_ob)
    banded_wide([jnp.transpose(w) for w in wm[::-1]], HID, t_mb)
    banded_wide(wi[::-1], 4, t_ib)

    for buf in (h1, h2, l2, l1):
        for n in range(2):
            buf[n, 0:DEEP, :] = jnp.zeros((DEEP, WIDE), BF16)
            buf[n, (rows + 1) * DEEP : (rows + 2) * DEEP, :] = jnp.zeros((DEEP, WIDE), BF16)
    for buf in (src, cc):
        for n in range(2):
            buf[n, 0:16, :] = jnp.zeros((16, WIDE), BF16)
            buf[n, (rows + 1) * 16 : (rows + 2) * 16, :] = jnp.zeros((16, WIDE), BF16)
    sixteen[...] = jnp.zeros_like(sixteen)
    lap[...] = jnp.zeros_like(lap)

    def inside(per_row, count, first):
        if halo == 0:
            return None
        at = lax.broadcasted_iota(jnp.int32, (count, WIDE), 0) // per_row + first
        at = at + (group * GROUP - halo) * 4
        return ((at >= 0) & (at < n_lat * 4)).astype(F32)

    def clear(v, per_row, first):
        if halo == 0:
            return v
        return v * inside(per_row, v.shape[0], first)

    for w in range(blocks):
        for which in range(3):
            pltpu.make_async_copy(*ends(0, w, which), x_recv.at[w, which]).wait()
    for w in range(blocks):
        before, after = ebuf[w, 0].astype(F32), ebuf[w, 1].astype(F32)
        side = jnp.concatenate(
            [
                jnp.where(low, after, before),
                pltpu.roll(jnp.where(low, before, after), TILE // 2, 1),
            ],
            axis=0,
        )
        both = dot(spread, jnp.concatenate([rbuf[w], side.astype(BF16)], axis=1))
        here = slice(w * 16, (w + 1) * 16)
        st[here, :] = clear(both[0:16], 4, 4 * w)
        fo[here, :] = both[16:32]
        se[here, :] = both[32:48]
        ka[here, :] = both[48:64]
        ma[here, :] = clear(both[64:80], 4, 4 * w)

    def put_narrow(target, n, v):
        for b, moved in enumerate((left_of(v), v, right_of(v))):
            for r in range(rows):
                sixteen[r * 16 + b * 4 : r * 16 + b * 4 + 4, :] = moved[r * 4 : r * 4 + 4]
        target[n, 16 : 16 + rows * 16, :] = sixteen[...].astype(BF16)

    def put_wide(target, n, w, v):
        v = clear(v, HID, 4 * w)
        for b, moved in enumerate((left_of(v), v, right_of(v))):
            moved = moved.astype(BF16)
            for r in range(4):
                top = (4 * w + r + 1) * DEEP + b * HID
                target[n, top : top + HID, :] = moved[r * HID : (r + 1) * HID]

    def centre(target, n, w):
        parts = []
        for r in range(4):
            top = (4 * w + r + 1) * DEEP + HID
            parts.append(target[n, top : top + HID, :])
        return jnp.concatenate(parts, axis=0).astype(F32)

    def narrow_window(target, n, w):
        return target[n, w * 64 : w * 64 + 96, :]

    def wide_window(target, n, w):
        return target[n, 4 * w * DEEP : 4 * w * DEEP + 6 * DEEP, :]

    def laplace(v):
        lap[8 : 8 + rows * 4, :] = v
        up = lap[4 : 4 + rows * 4, :]
        down = lap[12 : 12 + rows * 4, :]
        return up + down + left_of(v) + right_of(v) - 4.0 * v

    def forward(n, state):
        put_narrow(src, n, state)
        for w in range(blocks):
            put_wide(h1, n, w, jnp.tanh(dot(t_if[...], narrow_window(src, n, w))))
        for w in range(blocks):
            put_wide(h2, n, w, jnp.tanh(dot(t_mf[...], wide_window(h1, n, w))))
        closure = jnp.concatenate(
            [dot(t_of[...], wide_window(h2, n, w)) for w in range(blocks)], axis=0
        )
        return ma[...] * (state + ka[...] * laplace(state) + GAIN * closure + fo[...])

    def strip_wide(target, n):
        parts = []
        for s in range(OWN_ROWS + 2):
            top = (4 * halo + s) * DEEP
            parts.append(target[n, top : top + DEEP, 0:TILE])
        return jnp.concatenate(parts, axis=1)

    def strip_narrow(target, n):
        parts = []
        for s in range(OWN_ROWS + 2):
            top = (4 * halo + s) * 16
            parts.append(target[n, top : top + 16, 0:TILE])
        return jnp.concatenate(parts, axis=1)

    def strip_shifted(read, height):
        zero = jnp.zeros((height, TILE), BF16)
        cells = [read(r) for r in range(OWN_ROWS)]
        return jnp.concatenate(
            [jnp.concatenate([zero] * a + cells + [zero] * (2 - a), axis=1) for a in range(3)],
            axis=0,
        )

    def read_wide(target, n):
        def read(r):
            top = (4 * halo + r + 1) * DEEP + HID
            return target[n, top : top + HID, 0:TILE]

        return read

    def read_narrow(target, n):
        def read(r):
            top = (4 * halo + r + 1) * 16
            return target[n, top : top + 16, 0:TILE]

        return read

    def backward(n, masked, need_state):
        put_narrow(cc, n, GAIN * masked)
        grad_out = dot_nt(strip_shifted(read_narrow(cc, n), 16), strip_wide(h2, n))
        for w in range(blocks):
            slope = 1.0 - jnp.square(centre(h2, n, w))
            put_wide(l2, n, w, dot(t_ob[...], narrow_window(cc, n, w)) * slope)
        grad_mid = dot_nt(strip_shifted(read_wide(l2, n), HID), strip_wide(h1, n))
        for w in range(blocks):
            slope = 1.0 - jnp.square(centre(h1, n, w))
            put_wide(l1, n, w, dot(t_mb[...], wide_window(l2, n, w)) * slope)
        grad_in = dot_nt(strip_narrow(src, n), strip_shifted(read_wide(l1, n), HID))
        earlier = None
        if need_state:
            through = jnp.concatenate(
                [dot(t_ib[...], wide_window(l1, n, w)) for w in range(blocks)], axis=0
            )
            earlier = masked + laplace(ka[...] * masked) + through
        return earlier, (grad_in, grad_mid, grad_out)

    state = forward(0, st[...])
    final = forward(1, state)
    for i in range(GROUP):
        top = (halo + i) * 16
        fsrc[i] = final[top : top + 16, 0:TILE]
    for s in (1, 2, 3):
        i = (j + s) % GROUP
        copy = pltpu.make_async_remote_copy(
            src_ref=fsrc.at[i],
            dst_ref=fdst.at[j],
            send_sem=f_send.at[s],
            recv_sem=f_recv.at[j],
            device_id={"lat": group * GROUP + i, "lon": lon},
            device_id_type=MESH,
        )
        copy.start()
        waits.append((copy, None))
    pltpu.make_async_copy(fsrc.at[j], fdst.at[j], f_recv.at[j]).start()

    adjoint, late = backward(1, ma[...] * se[...], True)
    _, early = backward(0, ma[...] * adjoint, False)

    g_in, g_mid, g_out = (a + b for a, b in zip(late, early))
    acc[...] = jnp.zeros_like(acc)
    acc[0:96, 0:96] = g_mid * scale
    for a in range(3):
        acc[96 + a * 4 : 100 + a * 4, 0:96] = g_out[a * 16 + 4 : a * 16 + 8] * scale
    acc[108:120, 0:96] = g_in[0:12] * scale

    if reduce_here:
        rank = lon * n_lat + lat
        sums = []
        for o, (to_lat, to_lon) in enumerate(peer_ids):
            other = to_lon * n_lat + to_lat
            copy = pltpu.make_async_remote_copy(
                src_ref=acc.at[pl.ds(pl.multiple_of(other * 8, 8), 8)],
                dst_ref=rs.at[o],
                send_sem=rs_send.at[o],
                recv_sem=rs_recv.at[o],
                device_id={"lat": to_lat, "lon": to_lon},
                device_id_type=MESH,
            )
            copy.start()
            waits.append((copy, None))
            sums.append(copy)
        mine = pl.ds(pl.multiple_of(rank * 8, 8), 8)
        whole = acc[mine, :]
        for o, copy in enumerate(sums):
            copy.wait_recv()
            whole = whole + rs[o]
        chunk[...] = whole
        total[mine, :] = whole
        gathered = []
        for o, (to_lat, to_lon) in enumerate(peer_ids):
            copy = pltpu.make_async_remote_copy(
                src_ref=chunk,
                dst_ref=total.at[mine],
                send_sem=ag_send.at[o],
                recv_sem=ag_recv.at[o],
                device_id={"lat": to_lat, "lon": to_lon},
                device_id_type=MESH,
            )
            copy.start()
            waits.append((copy, None))
            gathered.append(copy)

    for i in range(GROUP):
        pltpu.make_async_copy(fsrc.at[0], fdst.at[i], f_recv.at[i]).wait()
    for i in range(GROUP):
        for r in range(4):
            final_ref[:, r, i * TILE : (i + 1) * TILE] = fdst[i, r * 4 : r * 4 + 4, :]
    stores = [pltpu.make_async_copy(final_ref, final_hbm, out_sem.at[0])]
    stores[0].start()

    if reduce_here:
        for copy in gathered:
            copy.wait_recv()
        result = total[...]
    else:
        result = acc[...]
    for a in range(3):
        for b in range(3):
            k = a * 3 + b
            side = slice(b * HID, (b + 1) * HID)
            gmid_ref[k] = result[a * HID : (a + 1) * HID, side]
            gout_ref[k] = result[96 + a * 4 : 100 + a * 4, side]
            gin_ref[k] = result[108 + b * 4 : 112 + b * 4, a * HID : (a + 1) * HID]
    for i, (here, there) in enumerate(
        ((gin_ref, gin_hbm), (gmid_ref, gmid_hbm), (gout_ref, gout_hbm))
    ):
        stores.append(pltpu.make_async_copy(here, there, out_sem.at[i + 1]))
        stores[-1].start()
    for copy, when in waits:
        if when is None:
            copy.wait_send()
        else:
            pl.when(when)(copy.wait_send)
    for store in stores:
        store.wait()


def hand_on(*refs):
    there, back, held, sems = refs[:4], refs[4:8], refs[8:12], refs[12]
    reads = [pltpu.make_async_copy(there[i], held[i], sems.at[0, i]) for i in range(4)]
    writes = [pltpu.make_async_copy(held[i], back[i], sems.at[1, i]) for i in range(4)]
    for read in reads:
        read.start()
    for read, write in zip(reads, writes):
        read.wait()
        write.start()
    for write in writes:
        write.wait()


def on_device(
    n_lat, n_lon,
    tracers, forcing, diffusivity, ocean_mask, weight_in, weight_mid, weight_out, sensitivity,
):
    halo = 0 if n_lat == GROUP else 3
    blocks = GROUP + 2 * halo
    rows = 4 * blocks
    scale = 1.0 / math.sqrt(tracers.shape[1] * n_lat * tracers.shape[2] * n_lon)
    sends = 12 if halo == 0 else 36
    wi = weight_in.transpose(2, 3, 1, 0).reshape(9, 4, HID)
    wm = weight_mid.transpose(2, 3, 0, 1).reshape(9, HID, HID)
    wo = weight_out.transpose(2, 3, 0, 1).reshape(9, 4, HID)
    field = pltpu.VMEM((rows * 4, WIDE), F32)
    wide = pltpu.VMEM((2, (rows + 2) * DEEP, WIDE), BF16)
    narrow = pltpu.VMEM((2, (rows + 2) * 16, WIDE), BF16)
    hbm = pl.BlockSpec(memory_space=pltpu.HBM)
    outs = (
        jax.ShapeDtypeStruct((4, 4, 512), F32),
        jax.ShapeDtypeStruct((9, 4, HID), F32),
        jax.ShapeDtypeStruct((9, HID, HID), F32),
        jax.ShapeDtypeStruct((9, 4, HID), F32),
    )
    final, g_in, g_mid, g_out = pl.pallas_call(
        functools.partial(kernel, n_lat, n_lon, halo, scale),
        out_shape=outs,
        in_specs=[hbm] * 8,
        out_specs=(hbm,) * 4,
        scratch_shapes=[pltpu.VMEM(o.shape, F32) for o in outs]
        + [
            pltpu.SemaphoreType.DMA((4,)),
            pltpu.VMEM((4, 4, 512), F32),
            pltpu.VMEM((4, 4, 512), F32),
            pltpu.VMEM((4, 512), F32),
            pltpu.VMEM((4, 512), jnp.int32),
            pltpu.VMEM((9, 4, HID), BF16),
            pltpu.VMEM((9, HID, HID), BF16),
            pltpu.VMEM((9, 4, HID), BF16),
            pltpu.VMEM((4, 4, 512), F32),
            pltpu.SemaphoreType.DMA((8,)),
            pltpu.VMEM((GROUP, 64, TILE), BF16),
            pltpu.VMEM((GROUP, 2, 32, TILE), BF16),
            pltpu.VMEM((blocks, 64, TILE), BF16),
            pltpu.VMEM((blocks, 2, 32, TILE), BF16),
            field, field, field, field, field,
            pltpu.VMEM((rows * 4 + 16, WIDE), F32),
            pltpu.VMEM((rows * 16, WIDE), F32),
            pltpu.VMEM((128, 96), BF16),
            pltpu.VMEM((16, 576), BF16),
            pltpu.VMEM((128, 576), BF16),
            pltpu.VMEM((128, 576), BF16),
            pltpu.VMEM((16, 576), BF16),
            pltpu.VMEM((128, 96), BF16),
            pltpu.VMEM((128, 640), F32),
            pltpu.VMEM((64, 512), F32),
            narrow, narrow, wide, wide, wide, wide,
            pltpu.VMEM((128, 128), F32),
            pltpu.VMEM((8, 128), F32),
            pltpu.VMEM((15, 8, 128), F32),
            pltpu.VMEM((128, 128), F32),
            pltpu.VMEM((GROUP, 16, TILE), F32),
            pltpu.VMEM((GROUP, 16, TILE), F32),
            pltpu.SemaphoreType.DMA((sends,)),
            pltpu.SemaphoreType.DMA((blocks, 3)),
            pltpu.SemaphoreType.DMA((GROUP,)),
            pltpu.SemaphoreType.DMA((GROUP,)),
            pltpu.SemaphoreType.DMA((15,)),
            pltpu.SemaphoreType.DMA((15,)),
            pltpu.SemaphoreType.DMA((15,)),
            pltpu.SemaphoreType.DMA((15,)),
        ],
        compiler_params=pltpu.CompilerParams(
            collective_id=0, has_side_effects=True, vmem_limit_bytes=VMEM_GRANT
        ),
    )(tracers, forcing, diffusivity, ocean_mask, wi, wm, wo, sensitivity)
    if n_lat * n_lon != 16:
        g_in, g_mid, g_out = lax.psum((g_in, g_mid, g_out), ("lon", "lat"))
    final, g_in, g_mid, g_out = pl.pallas_call(
        hand_on,
        out_shape=outs,
        in_specs=[hbm] * 4,
        out_specs=(hbm,) * 4,
        scratch_shapes=[pltpu.VMEM(o.shape, F32) for o in outs]
        + [pltpu.SemaphoreType.DMA((2, 4))],
        compiler_params=pltpu.CompilerParams(vmem_limit_bytes=VMEM_GRANT),
    )(final, g_in, g_mid, g_out)
    return (
        final,
        g_in.reshape(3, 3, 4, HID).transpose(3, 2, 0, 1),
        g_mid.reshape(3, 3, HID, HID).transpose(2, 3, 0, 1),
        g_out.reshape(3, 3, 4, HID).transpose(2, 3, 0, 1),
    )


def solution(mesh):
    field = P("ens", "lat", "lon")
    cells = P("lat", "lon")
    gradient = P("ens", None, None, None)
    return jax.shard_map(
        functools.partial(on_device, mesh.shape["lat"], mesh.shape["lon"]),
        mesh=mesh,
        in_specs=(field, field, cells, cells, P(), P(), P(), field),
        out_specs=(field, gradient, gradient, gradient),
        check_vma=False,
    )
```
